256 devices in a mesh: blk: 16 (over x, y_lo, core), tm: 16 (over y_hi, z).
Axes of the slice: x: 4, y: 4 (y_hi: 2, y_lo: 2; y = y_hi * 2 + y_lo), z: 8, core: 2. Of those that a mesh axis runs over, the one named last changes fastest.
Arguments:
- readings: bfloat16 [65536, 16384], P('blk', 'tm'), may hold values from -6 to 6
- tile_mask: int32 [512, 128], P('blk', 'tm'), may hold values 0 or 1
- sensor_f: bfloat16 [65536, 256], P('blk'), may hold values from -6 to 6
- time_f: bfloat16 [16384, 256], P('tm'), may hold values from -6 to 6
- ar_weight: float32 [3, 256], replicated, may hold values from 0.1 to 0.45
Outputs:
- new_sensor_f: bfloat16 [65536, 256], P('blk')
- new_time_f: bfloat16 [16384, 256], P('tm')
The draws below stay inside these ranges and needn't reach their ends.
All inputs are finite; a program needn't handle non-finite values. No bound on the sum of `tile_mask` on one device may be relied on, other than what follows from the above.
Results may differ from the reference program's by a relative error of at most 0.0041.
Values may be sent and summed in bfloat16 or wider, within the bound.
A program may use at most 128 MiB of HBM per device.

```python
import math
import jax
import jax.numpy as jnp

RANK = 256
TILE = 128
LAG = 96
SENS = 65536
TIME = 16384


def set_ends(drawn, own_key, smallest, high):
    longest = drawn.shape.index(max(drawn.shape))
    spots = []
    for shift in (0, 1):
        where = [jax.random.randint(jax.random.fold_in(own_key, axis), (), 0, length) for axis, length in enumerate(drawn.shape)]
        where[longest] = (where[longest] + shift) % drawn.shape[longest]
        spots.append(tuple(where))
    return drawn.at[spots[0]].set(smallest).at[spots[1]].set(high)


def block_scale(stream_key, extent, shards, least, top_value):
    def one(position, shards_of):
        draws = jax.random.uniform(jax.random.fold_in(jax.random.fold_in(stream_key, 6), position), (shards_of,), jnp.float32, least / len(shards), top_value / len(shards))
        return jnp.repeat(jnp.exp(draws), extent[position] // shards_of).reshape((-1,) + (1,) * (len(extent) - position - 1))

    gain = one(*shards[0])
    for cut in shards[1:]:
        gain = gain * one(*cut)
    return gain


def bell_draw(stream_key, extent, spread, reach, cuts=(), dtype=jnp.bfloat16):
    drawn = spread * jax.random.normal(stream_key, extent, jnp.float32)
    if cuts:
        drawn = drawn * block_scale(stream_key, extent, cuts, -0.22, 0.18)
    return jnp.clip(drawn, -reach, reach).astype(dtype)


def setup_inputs(seed: int = 0) -> dict:
    arg_keys = jax.random.split(jax.random.key(seed), 6)
    return {
        "readings": bell_draw(arg_keys[0], (SENS, TIME), 1.0, 6.0, ((0, 16), (1, 16))),
        "tile_mask": set_ends((jax.random.randint(arg_keys[1], (SENS // TILE, TIME // TILE), 0, 8) < 1).astype(jnp.int32), jax.random.fold_in(arg_keys[1], 1), 0, 1),
        "sensor_f": bell_draw(arg_keys[2], (SENS, RANK), 1.0, 6.0, ((0, 16),)),
        "time_f": bell_draw(arg_keys[3], (TIME, RANK), 1.0, 6.0, ((0, 16),)),
        "ar_weight": jnp.clip(jax.random.uniform(arg_keys[4], (3, RANK), jnp.float32, 0.1, 0.45), 0.1, 0.45),
    }


def shift_later(values, lag):
    pad = jnp.zeros((lag, values.shape[1]), jnp.float32)
    return jnp.concatenate([pad, values[:-lag]], axis=0)

def shift_earlier(values, lag):
    pad = jnp.zeros((lag, values.shape[1]), jnp.float32)
    return jnp.concatenate([values[lag:], pad], axis=0)

def reference(readings, tile_mask, sensor_f, time_f, ar_weight):
    scale = 1.0 / math.sqrt(RANK)
    pred = jnp.dot(sensor_f, time_f.T, preferred_element_type=jnp.float32) * scale
    rows, cols = readings.shape
    diff = (readings.astype(jnp.float32) - pred).reshape(rows // TILE, TILE, cols // TILE, TILE)
    keep = tile_mask.astype(jnp.float32)[:, None, :, None]
    resid = (diff * keep).reshape(rows, cols).astype(jnp.bfloat16)
    grad_s = jnp.dot(resid, time_f, preferred_element_type=jnp.float32) * scale
    grad_t = jnp.dot(resid.T, sensor_f, preferred_element_type=jnp.float32) * scale
    lags = (1, 12, LAG)
    factor = time_f.astype(jnp.float32)
    ar_err = factor
    for index in range(3):
        ar_err = ar_err - ar_weight[index] * shift_later(factor, lags[index])
    ar_adj = ar_err
    for index in range(3):
        ar_adj = ar_adj - ar_weight[index] * shift_earlier(ar_err, lags[index])
    new_sensor_f = (0.9 * sensor_f.astype(jnp.float32) + 2.0 * math.sqrt(RANK / TIME) * grad_s).astype(jnp.bfloat16)
    new_time_f = (factor + 2.0 * math.sqrt(RANK / SENS) * grad_t - 0.5 * ar_adj).astype(jnp.bfloat16)
    return (new_sensor_f, new_time_f)
```

```python
import functools
import math

import jax
import jax.numpy as jnp
from jax import lax
from jax.experimental import pallas as pl
from jax.experimental.pallas import tpu as pltpu
from jax.sharding import PartitionSpec as P

TILE = 128
LAG = 96
RANK = 256
GROUP = 4 * TILE
COLS = 256
MESH = pl.DeviceIdType.MESH
F32 = jnp.float32
BF16 = jnp.bfloat16
HALF = TILE // 2

PLACE = {4: 0, 3: 1, 5: 2, 2: 3, 6: 4, 1: 5, 7: 6, 0: 7}


def kernel(
    step_sens, step_time,
    rd_hbm, mask, sn_hbm, t_hbm, arw,
    outs_hbm, outt_hbm,
    rd, sn, tpad, g, gtt, s_t, resid, ysend, yrecv, zsend, zru, zrd, pxs, pxr, out,
    gt, core_in, xs, xr, acc, ys, yr, winf, errf, tout,
    load_sem, store_sem, send_sem, recv_sem,
):
    blk = lax.axis_index("blk")
    tm = lax.axis_index("tm")
    x, ylo, c = blk // 4, (blk // 2) % 2, blk % 2
    h, z = tm // 8, tm % 8

    def at_blk(x_, ylo_, c_):
        return ((x_ * 2 + ylo_) * 2 + c_, tm)

    up = (blk, h * 8 + (z + 1) % 8)
    down = (blk, h * 8 + (z + 7) % 8)
    pair = (blk, (1 - h) * 8 + z)
    after = (blk, (tm + 1) % 16)
    before = (blk, (tm + 15) % 16)
    other_core = at_blk(x, ylo, 1 - c)
    x_away = [None] + [at_blk((x + d) % 4, ylo, c) for d in (1, 2, 3)]
    y_next = at_blk(x, 1 - ylo, c)

    barrier = pltpu.get_barrier_semaphore()
    partners = [up, down, pair, after, before, other_core, y_next] + x_away[1:]
    for who in partners:
        pl.semaphore_signal(barrier, inc=1, device_id=who, device_id_type=MESH)

    t_rows = t_hbm.shape[0]
    t_load = pltpu.make_async_copy(t_hbm, tpad.at[pl.ds(LAG, t_rows)], load_sem.at[16])

    def rows_of(k):
        return pl.multiple_of(((z + k) % 8) * GROUP, GROUP)

    def owner_of(p):
        d = (p + 1) // 2
        return (z + 8 + 4 + d * (1 - 2 * (p % 2))) % 8

    def loads(p):
        r = pl.multiple_of(owner_of(p) * GROUP, GROUP)
        a = pltpu.make_async_copy(sn_hbm.at[pl.ds(r, GROUP)], sn.at[pl.ds(r, GROUP)], load_sem.at[p])
        b = pltpu.make_async_copy(rd_hbm.at[pl.ds(r, GROUP)], rd.at[pl.ds(r, GROUP)], load_sem.at[8 + p])
        return a, b

    t_load.start()
    for p in range(8):
        for cp in loads(p):
            cp.start()

    q_off = [h * TILE, (1 - h) * TILE, (2 + h) * TILE, (3 - h) * TILE]
    q_off = [pl.multiple_of(v, TILE) for v in q_off]

    def q_rows(q):
        return pl.ds(q_off[q], TILE)

    count = [8]
    sent = []

    def message(src, dst, who):
        n = count[0]
        count[0] += 1
        return pltpu.make_async_remote_copy(
            src_ref=src, dst_ref=dst, send_sem=send_sem.at[n], recv_sem=recv_sem.at[n],
            device_id=who, device_id_type=MESH,
        )

    def start(msg):
        msg.start()
        sent.append(msg)

    def y_message(p):
        return pltpu.make_async_remote_copy(
            src_ref=ysend.at[p], dst_ref=yrecv.at[p], send_sem=send_sem.at[p], recv_sem=recv_sem.at[p],
            device_id=pair, device_id_type=MESH,
        )

    gtt[...] = jnp.zeros_like(gtt)

    def compute(p):
        o = owner_of(p)
        r = pl.multiple_of(o * GROUP, GROUP)
        for cp in loads(p):
            cp.wait()
        s = sn[pl.ds(r, GROUP), :]
        s_t[...] = s.T
        g[p] = jnp.zeros((GROUP, RANK), F32)

        def columns(j, carry):
            col = pl.multiple_of(j * COLS, COLS)
            tj = tpad[pl.ds(LAG + col, COLS), :]
            pred = lax.dot_general(
                sn[pl.ds(r, GROUP), :], tj, (((1,), (1,)), ((), ())), preferred_element_type=F32
            )
            diff = rd[pl.ds(r, GROUP), pl.ds(col, COLS)].astype(F32) - pred * (1.0 / math.sqrt(RANK))
            for i in range(GROUP // TILE):
                for jj in range(COLS // TILE):
                    keep = mask[o * (GROUP // TILE) + i, j * (COLS // TILE) + jj].astype(F32)
                    block = diff[i * TILE : (i + 1) * TILE, jj * TILE : (jj + 1) * TILE]
                    resid[i * TILE : (i + 1) * TILE, jj * TILE : (jj + 1) * TILE] = (block * keep).astype(BF16)
            left = resid[...]
            g[p] += jnp.dot(left, tj, preferred_element_type=F32)
            gtt[:, pl.ds(col, COLS)] += jnp.dot(s_t[...], left, preferred_element_type=F32)
            return carry

        lax.fori_loop(0, t_rows // COLS, columns, 0)

    def y_first(p):
        ysend[p] = g[p, q_rows(3), :].astype(BF16)
        y_message(p).start()

    def compute_some(first, last):
        def one(p, carry):
            compute(p)
            y_first(p)
            return carry

        lax.fori_loop(first, last, one, 0)

    z_up, z_down = {}, {}
    for k in (4, 3, 2, 1):
        for q in range(3):
            p, p_down = PLACE[k], PLACE[(8 - k) % 8]
            a, b = q * TILE, (q + 1) * TILE
            if k == 4:
                if q == 0:
                    z_up[k, q] = message(zsend.at[p, a:b], zru.at[k - 1, a:b], up)
                elif q == 1:
                    z_down[k, q] = message(zsend.at[p, a:b], zrd.at[k - 1, a:b], down)
                else:
                    z_up[k, q] = message(zsend.at[p, a : a + HALF], zru.at[k - 1, a : a + HALF], up)
                    z_down[k, q] = message(zsend.at[p, a + HALF : b], zrd.at[k - 1, a + HALF : b], down)
            else:
                z_up[k, q] = message(zsend.at[p, a:b], zru.at[k - 1, a:b], up)
                z_down[k, q] = message(zsend.at[p_down, a:b], zrd.at[k - 1, a:b], down)

    def own(p, q):
        part = g[p, q_rows(q), :]
        if q == 2:
            part = part + yrecv[p].astype(F32)
        return part

    def pass_on(k, q, upward):
        p = PLACE[k] if upward else PLACE[(8 - k) % 8]
        a, b = q * TILE, (q + 1) * TILE
        table, landed = (z_up, zru) if upward else (z_down, zrd)
        if q == 2 and (k == 4 and upward or k < 4):
            y_message(p).wait_recv()
        part = own(p, q)
        if k < 4 and (k + 1, q) in table:
            table[k + 1, q].wait_recv()
            if k == 3 and q == 2:
                if upward:
                    lo = part[:HALF] + landed[k, a : a + HALF].astype(F32)
                    part = jnp.concatenate([lo, part[HALF:]], axis=0)
                else:
                    hi = part[HALF:] + landed[k, a + HALF : b].astype(F32)
                    part = jnp.concatenate([part[:HALF], hi], axis=0)
            else:
                part = part + landed[k, a:b].astype(F32)
        if k == 4 and q == 2:
            if upward:
                zsend[p, a : a + HALF] = part[:HALF].astype(BF16)
            else:
                zsend[p, a + HALF : b] = part[HALF:].astype(BF16)
        else:
            zsend[p, a:b] = part.astype(BF16)
        start(table[k, q])

    t_load.wait()
    compute(0)
    pl.semaphore_wait(barrier, len(partners))
    y_first(0)
    pass_on(4, 0, True)
    pass_on(4, 1, False)
    rim_up = message(tpad.at[pl.ds(t_rows, LAG)], tpad.at[pl.ds(0, LAG)], after)
    rim_down = message(tpad.at[pl.ds(LAG, LAG)], tpad.at[pl.ds(LAG + t_rows, LAG)], before)
    start(rim_up)
    start(rim_down)
    compute_some(1, 3)
    pass_on(3, 1, True)
    pass_on(3, 0, False)
    pass_on(4, 2, True)
    pass_on(4, 2, False)
    pass_on(3, 0, True)
    pass_on(3, 1, False)
    compute_some(3, 5)
    pass_on(3, 2, True)
    pass_on(3, 2, False)
    for q in (1, 0):
        pass_on(2, q, True)
        pass_on(2, 1 - q, False)
    compute_some(5, 8)

    for j in range(t_rows // COLS):
        gt[j * COLS : (j + 1) * COLS, :] = gtt[:, j * COLS : (j + 1) * COLS].T
    half_t = t_rows // 2
    per_x = half_t // 4
    per_y = per_x // 2
    mine = pl.multiple_of(c * half_t, half_t)
    theirs = pl.multiple_of((1 - c) * half_t, half_t)
    core_msg = message(gt.at[pl.ds(theirs, half_t)], core_in, other_core)
    start(core_msg)

    pass_on(2, 2, True)
    pass_on(2, 2, False)
    for q in (1, 0):
        pass_on(1, q, True)
        pass_on(1, 1 - q, False)

    def x_rows(d):
        return pl.multiple_of(((x + d) % 4) * per_x, per_x)

    core_msg.wait_recv()
    x_msgs = []
    for d in (1, 2, 3):
        r = x_rows(d)
        xs[d - 1] = (gt[pl.ds(mine + r, per_x), :] + core_in[pl.ds(r, per_x), :]).astype(BF16)
        msg = message(xs.at[d - 1], xr.at[d - 1], x_away[d])
        start(msg)
        x_msgs.append(msg)
    r = x_rows(0)
    acc[...] = gt[pl.ds(mine + r, per_x), :] + core_in[pl.ds(r, per_x), :]

    pass_on(1, 2, True)
    pass_on(1, 2, False)

    def z_total(q):
        if q == 2:
            y_message(7).wait_recv()
        part = own(7, q)
        a, b = q * TILE, (q + 1) * TILE
        z_up[1, q].wait_recv()
        part = part + zru[0, a:b].astype(F32)
        z_down[1, q].wait_recv()
        return part + zrd[0, a:b].astype(F32)

    def out_rows(k, q):
        return pl.multiple_of(rows_of(k) + q_off[q], TILE)

    def finished(q, total):
        r = out_rows(0, q)
        sensors = sn[pl.ds(r, TILE), :].astype(F32)
        out[pl.ds(r, TILE), :] = (0.9 * sensors + (step_sens / math.sqrt(RANK)) * total).astype(BF16)

    g_up, g_down, g_pair = {}, {}, {}

    def hand_on(s, q):
        for upward in (True, False):
            k = (8 - (s - 1)) % 8 if upward else s - 1
            r = out_rows(k, q)
            table, who = (g_up, up) if upward else (g_down, down)
            size = TILE
            if s == 4:
                if q == 0 and not upward or q == 1 and upward:
                    continue
                if q == 2:
                    size = HALF
                    r = r if upward else r + HALF
            if s > 1:
                table[s - 1, q].wait_recv()
            rows = out.at[pl.ds(r, size)]
            table[s, q] = message(rows, rows, who)
            start(table[s, q])
            if q == 2 and (s == 1 and upward or s > 1):
                across(k, (8 - k) % 8 if k else 0)

    def across(k, label):
        r = out_rows(k, 2)
        rows = out.at[pl.ds(r, TILE)]
        g_pair[k] = message(rows, rows, pair)
        start(g_pair[k])

    pxs[...] = z_total(1).astype(BF16)
    px_msg = message(pxs, pxr, pair)
    start(px_msg)
    g[7, q_rows(0), :] = z_total(0)
    finished(2, z_total(2))
    hand_on(1, 2)

    for msg in x_msgs:
        msg.wait_recv()
    acc[...] += (xr[0].astype(F32) + xr[1].astype(F32)) + xr[2].astype(F32)
    ys[...] = acc[pl.ds(pl.multiple_of((1 - ylo) * per_y, per_y), per_y), :].astype(BF16)
    y_msg = message(ys, yr, y_next)
    start(y_msg)

    px_msg.wait_recv()
    finished(0, g[7, q_rows(0), :] + pxr[...].astype(F32))
    r0 = out_rows(0, 0)
    fin_msg = message(out.at[pl.ds(r0, TILE)], out.at[pl.ds(r0, TILE)], pair)
    start(fin_msg)
    hand_on(1, 0)
    hand_on(2, 2)

    rim_up.wait_recv()
    rim_down.wait_recv()
    y_msg.wait_recv()
    first = pl.multiple_of(mine + x_rows(0) + ylo * per_y, per_y)
    seen = per_y + 2 * LAG
    win = tpad[pl.ds(first, seen), :].astype(F32)
    step = first - LAG + lax.broadcasted_iota(jnp.int32, (seen, RANK), 0)
    winf[...] = jnp.where((step >= 0) | (tm > 0), win, 0.0)
    errs = per_y + LAG
    err = winf[LAG : LAG + errs, :]
    lags = (1, 12, LAG)
    for i in range(3):
        err = err - arw[i : i + 1, :] * winf[LAG - lags[i] : LAG - lags[i] + errs, :]
    step = first + lax.broadcasted_iota(jnp.int32, (errs, RANK), 0)
    errf[...] = jnp.where((step < t_rows) | (tm < 15), err, 0.0)
    adj = errf[0:per_y, :]
    for i in range(3):
        adj = adj - arw[i : i + 1, :] * errf[lags[i] : lags[i] + per_y, :]
    total = acc[pl.ds(pl.multiple_of(ylo * per_y, per_y), per_y), :] + yr[...].astype(F32)
    new = winf[LAG : LAG + per_y, :] + (step_time / math.sqrt(RANK)) * total - 0.5 * adj
    tout[pl.ds(first, per_y), :] = new.astype(BF16)
    ty_rows = tout.at[pl.ds(first, per_y)]
    ty_msg = message(ty_rows, ty_rows, y_next)
    start(ty_msg)

    fin_msg.wait_recv()
    hand_on(1, 1)
    hand_on(2, 0)
    hand_on(3, 2)
    ty_msg.wait_recv()
    tx_rows = tout.at[pl.ds(pl.multiple_of(mine + x_rows(0), per_x), per_x)]
    tx_msgs = []
    for d in (1, 2, 3):
        msg = message(tx_rows, tx_rows, x_away[d])
        start(msg)
        tx_msgs.append(msg)
    hand_on(2, 1)
    hand_on(3, 0)
    hand_on(4, 2)
    hand_on(3, 1)
    hand_on(4, 0)
    hand_on(4, 1)
    for msg in tx_msgs:
        msg.wait_recv()
    tc_rows = tout.at[pl.ds(mine, half_t)]
    tc_msg = message(tc_rows, tc_rows, other_core)
    start(tc_msg)

    g_up[4, 2].wait_recv()
    g_down[4, 2].wait_recv()
    across(4, 4)
    stores = []

    def store(src, dst):
        cp = pltpu.make_async_copy(src, dst, store_sem.at[len(stores)])
        cp.start()
        stores.append(cp)

    tc_msg.wait_recv()
    store(tout, outt_hbm)
    g_up[4, 0].wait_recv()
    g_down[4, 1].wait_recv()
    for s in (3,):
        for q in (0, 1):
            if q == 0:
                g_down[3, 0].wait_recv()
            else:
                g_up[3, 1].wait_recv()
    for k in (0, 7, 1, 6, 2, 5, 3, 4):
        g_pair[k].wait_recv()
        rows = pl.ds(rows_of(k), GROUP)
        store(out.at[rows], outs_hbm.at[rows])
    for p in range(8):
        y_message(p).wait_send()
    for msg in sent:
        msg.wait_send()
    for cp in stores:
        cp.wait()


def on_device(readings, tile_mask, sensor_f, time_f, ar_weight):
    sens_here, time_here = readings.shape
    time_total = time_here * lax.axis_size("tm")
    sens_total = sens_here * lax.axis_size("blk")
    rank = sensor_f.shape[1]
    step_sens = 2.0 * math.sqrt(rank / time_total)
    step_time = 2.0 * math.sqrt(rank / sens_total)
    half_t = time_here // 2
    per_x = half_t // 4
    per_y = per_x // 2
    anywhere = pl.BlockSpec(memory_space=pl.ANY)
    in_vmem = pl.BlockSpec(memory_space=pltpu.VMEM)
    messages = 100
    flops = 6 * sens_here * time_here * rank
    return pl.pallas_call(
        functools.partial(kernel, step_sens, step_time),
        out_shape=(
            jax.ShapeDtypeStruct(sensor_f.shape, BF16),
            jax.ShapeDtypeStruct(time_f.shape, BF16),
        ),
        in_specs=[anywhere, pl.BlockSpec(memory_space=pltpu.SMEM), anywhere, anywhere, in_vmem],
        out_specs=(anywhere, anywhere),
        scratch_shapes=[
            pltpu.VMEM((sens_here, time_here), BF16),
            pltpu.VMEM((sens_here, rank), BF16),
            pltpu.VMEM((time_here + 2 * LAG, rank), BF16),
            pltpu.VMEM((8, GROUP, rank), F32),
            pltpu.VMEM((rank, time_here), F32),
            pltpu.VMEM((rank, GROUP), BF16),
            pltpu.VMEM((GROUP, COLS), BF16),
            pltpu.VMEM((8, TILE, rank), BF16),
            pltpu.VMEM((8, TILE, rank), BF16),
            pltpu.VMEM((8, 3 * TILE, rank), BF16),
            pltpu.VMEM((4, 3 * TILE, rank), BF16),
            pltpu.VMEM((4, 3 * TILE, rank), BF16),
            pltpu.VMEM((TILE, rank), BF16),
            pltpu.VMEM((TILE, rank), BF16),
            pltpu.VMEM((sens_here, rank), BF16),
            pltpu.VMEM((time_here, rank), F32),
            pltpu.VMEM((half_t, rank), F32),
            pltpu.VMEM((3, per_x, rank), BF16),
            pltpu.VMEM((3, per_x, rank), BF16),
            pltpu.VMEM((per_x, rank), F32),
            pltpu.VMEM((per_y, rank), BF16),
            pltpu.VMEM((per_y, rank), BF16),
            pltpu.VMEM((per_y + 2 * LAG, rank), F32),
            pltpu.VMEM((per_y + LAG, rank), F32),
            pltpu.VMEM((time_here, rank), BF16),
            pltpu.SemaphoreType.DMA((17,)),
            pltpu.SemaphoreType.DMA((9,)),
            pltpu.SemaphoreType.DMA((messages,)),
            pltpu.SemaphoreType.DMA((messages,)),
        ],
        compiler_params=pltpu.CompilerParams(
            collective_id=0, has_side_effects=True, vmem_limit_bytes=48 * 1024 * 1024
        ),
        cost_estimate=pl.CostEstimate(
            flops=flops, bytes_accessed=2 * sens_here * time_here, transcendentals=0
        ),
        name="sweep",
    )(readings, tile_mask, sensor_f, time_f, ar_weight)


def solution(mesh):
    return jax.shard_map(
        on_device,
        mesh=mesh,
        in_specs=(P("blk", "tm"), P("blk", "tm"), P("blk", None), P("tm", None), P()),
        out_specs=(P("blk", None), P("tm", None)),
        check_vma=False,
    )
```

```python
import functools
import math

import jax
import jax.numpy as jnp
from jax import lax
from jax.experimental import pallas as pl
from jax.experimental.pallas import tpu as pltpu
from jax.sharding import PartitionSpec as P

TILE = 128
LAG = 96
RANK = 256
GROUP = 4 * TILE
COLS = 256
MESH = pl.DeviceIdType.MESH
F32 = jnp.float32
BF16 = jnp.bfloat16
HALF = TILE // 2

PLACE = {4: 0, 3: 1, 5: 2, 2: 3, 6: 4, 1: 5, 7: 6, 0: 7}


def kernel(
    step_sens, step_time,
    rd_hbm, mask_hbm, sn_hbm, t_hbm, arw_hbm,
    out, tout,
    mask, arw, rd, sn, tpad, t_t, g, gtt, s_t, resid, ysend, yrecv, zsend, zru, zrd, pxs, pxr,
    gt, core_in, xs, xr, acc, ys, yr, winf, errf,
    load_sem, send_sem, recv_sem,
):
    blk = lax.axis_index("blk")
    tm = lax.axis_index("tm")
    x, ylo, c = blk // 4, (blk // 2) % 2, blk % 2
    h, z = tm // 8, tm % 8

    def at_blk(x_, ylo_, c_):
        return ((x_ * 2 + ylo_) * 2 + c_, tm)

    up = (blk, h * 8 + (z + 1) % 8)
    down = (blk, h * 8 + (z + 7) % 8)
    pair = (blk, (1 - h) * 8 + z)
    after = (blk, (tm + 1) % 16)
    before = (blk, (tm + 15) % 16)
    other_core = at_blk(x, ylo, 1 - c)
    x_away = [None] + [at_blk((x + d) % 4, ylo, c) for d in (1, 2, 3)]
    y_next = at_blk(x, 1 - ylo, c)

    barrier = pltpu.get_barrier_semaphore()
    partners = [up, down, pair, after, before, other_core, y_next] + x_away[1:]
    for who in partners:
        pl.semaphore_signal(barrier, inc=1, device_id=who, device_id_type=MESH)

    t_rows = t_hbm.shape[0]
    t_load = pltpu.make_async_copy(t_hbm, tpad.at[pl.ds(LAG, t_rows)], load_sem.at[16])

    def rows_of(k):
        return pl.multiple_of(((z + k) % 8) * GROUP, GROUP)

    def owner_of(p):
        d = (p + 1) // 2
        return (z + 8 + 4 + d * (1 - 2 * (p % 2))) % 8

    def loads(p):
        r = pl.multiple_of(owner_of(p) * GROUP, GROUP)
        a = pltpu.make_async_copy(sn_hbm.at[pl.ds(r, GROUP)], sn.at[pl.ds(r, GROUP)], load_sem.at[p])
        b = pltpu.make_async_copy(rd_hbm.at[pl.ds(r, GROUP)], rd.at[pl.ds(r, GROUP)], load_sem.at[8 + p])
        return a, b

    mask_load = pltpu.make_async_copy(mask_hbm, mask, load_sem.at[17])
    arw_load = pltpu.make_async_copy(arw_hbm, arw, load_sem.at[18])
    t_load.start()
    mask_load.start()
    for p in range(8):
        for cp in loads(p):
            cp.start()
    arw_load.start()

    q_off = [h * TILE, (1 - h) * TILE, (2 + h) * TILE, (3 - h) * TILE]
    q_off = [pl.multiple_of(v, TILE) for v in q_off]

    def q_rows(q):
        return pl.ds(q_off[q], TILE)

    count = [8]
    sent = []

    def message(src, dst, who):
        n = count[0]
        count[0] += 1
        return pltpu.make_async_remote_copy(
            src_ref=src, dst_ref=dst, send_sem=send_sem.at[n], recv_sem=recv_sem.at[n],
            device_id=who, device_id_type=MESH,
        )

    def start(msg):
        msg.start()
        sent.append(msg)

    def y_message(p):
        return pltpu.make_async_remote_copy(
            src_ref=ysend.at[p], dst_ref=yrecv.at[p], send_sem=send_sem.at[p], recv_sem=recv_sem.at[p],
            device_id=pair, device_id_type=MESH,
        )

    gtt[...] = jnp.zeros_like(gtt)

    def compute(p):
        o = owner_of(p)
        r = pl.multiple_of(o * GROUP, GROUP)
        for cp in loads(p):
            cp.wait()
        s_t[...] = sn[pl.ds(r, GROUP), :].T
        for j in range(t_rows // COLS):
            cols = slice(j * COLS, (j + 1) * COLS)
            pred = jnp.dot(sn[pl.ds(r, GROUP), :], t_t[:, cols], preferred_element_type=F32)
            diff = rd[pl.ds(r, GROUP), cols].astype(F32) - pred * (1.0 / math.sqrt(RANK))
            for i in range(GROUP // TILE):
                for jj in range(COLS // TILE):
                    keep = mask[j * (COLS // TILE) + jj, o * (GROUP // TILE) + i].astype(F32)
                    block = diff[i * TILE : (i + 1) * TILE, jj * TILE : (jj + 1) * TILE]
                    a, b = i * TILE, j * COLS + jj * TILE
                    resid[a : a + TILE, b : b + TILE] = (block * keep).astype(BF16)
        g[p] = jnp.dot(resid[...], tpad[LAG : LAG + t_rows, :], preferred_element_type=F32)
        gtt[...] += jnp.dot(s_t[...], resid[...], preferred_element_type=F32)

    def y_first(p):
        ysend[p] = g[p, q_rows(3), :].astype(BF16)
        y_message(p).start()

    def compute_some(first, last):
        def one(p, carry):
            compute(p)
            y_first(p)
            return carry

        lax.fori_loop(first, last, one, 0)

    z_up, z_down = {}, {}
    for k in (4, 3, 2, 1):
        for q in range(3):
            p, p_down = PLACE[k], PLACE[(8 - k) % 8]
            a, b = q * TILE, (q + 1) * TILE
            if k == 4:
                if q == 0:
                    z_up[k, q] = message(zsend.at[p, a:b], zru.at[k - 1, a:b], up)
                elif q == 1:
                    z_down[k, q] = message(zsend.at[p, a:b], zrd.at[k - 1, a:b], down)
                else:
                    z_up[k, q] = message(zsend.at[p, a : a + HALF], zru.at[k - 1, a : a + HALF], up)
                    z_down[k, q] = message(zsend.at[p, a + HALF : b], zrd.at[k - 1, a + HALF : b], down)
            else:
                z_up[k, q] = message(zsend.at[p, a:b], zru.at[k - 1, a:b], up)
                z_down[k, q] = message(zsend.at[p_down, a:b], zrd.at[k - 1, a:b], down)

    def own(p, q):
        part = g[p, q_rows(q), :]
        if q == 2:
            part = part + yrecv[p].astype(F32)
        return part

    def pass_on(k, q, upward):
        p = PLACE[k] if upward else PLACE[(8 - k) % 8]
        a, b = q * TILE, (q + 1) * TILE
        table, landed = (z_up, zru) if upward else (z_down, zrd)
        if q == 2 and (k == 4 and upward or k < 4):
            y_message(p).wait_recv()
        part = own(p, q)
        if k < 4 and (k + 1, q) in table:
            table[k + 1, q].wait_recv()
            if k == 3 and q == 2:
                if upward:
                    lo = part[:HALF] + landed[k, a : a + HALF].astype(F32)
                    part = jnp.concatenate([lo, part[HALF:]], axis=0)
                else:
                    hi = part[HALF:] + landed[k, a + HALF : b].astype(F32)
                    part = jnp.concatenate([part[:HALF], hi], axis=0)
            else:
                part = part + landed[k, a:b].astype(F32)
        if k == 4 and q == 2:
            if upward:
                zsend[p, a : a + HALF] = part[:HALF].astype(BF16)
            else:
                zsend[p, a + HALF : b] = part[HALF:].astype(BF16)
        else:
            zsend[p, a:b] = part.astype(BF16)
        start(table[k, q])

    t_load.wait()
    t_t[...] = tpad[LAG : LAG + t_rows, :].T
    mask_load.wait()
    compute(0)
    pl.semaphore_wait(barrier, len(partners))
    y_first(0)
    pass_on(4, 0, True)
    pass_on(4, 1, False)
    rim_up = message(tpad.at[pl.ds(t_rows, LAG)], tpad.at[pl.ds(0, LAG)], after)
    rim_down = message(tpad.at[pl.ds(LAG, LAG)], tpad.at[pl.ds(LAG + t_rows, LAG)], before)
    start(rim_up)
    start(rim_down)
    compute_some(1, 3)
    pass_on(3, 1, True)
    pass_on(3, 0, False)
    pass_on(4, 2, True)
    pass_on(4, 2, False)
    pass_on(3, 0, True)
    pass_on(3, 1, False)
    compute_some(3, 5)
    pass_on(3, 2, True)
    pass_on(3, 2, False)
    for q in (1, 0):
        pass_on(2, q, True)
        pass_on(2, 1 - q, False)
    compute_some(5, 8)

    for j in range(t_rows // COLS):
        gt[j * COLS : (j + 1) * COLS, :] = gtt[:, j * COLS : (j + 1) * COLS].T
    half_t = t_rows // 2
    per_x = half_t // 4
    per_y = per_x // 2
    mine = pl.multiple_of(c * half_t, half_t)
    theirs = pl.multiple_of((1 - c) * half_t, half_t)
    core_msg = message(gt.at[pl.ds(theirs, half_t)], core_in, other_core)
    start(core_msg)

    pass_on(2, 2, True)
    pass_on(2, 2, False)
    for q in (1, 0):
        pass_on(1, q, True)
        pass_on(1, 1 - q, False)

    def x_rows(d):
        return pl.multiple_of(((x + d) % 4) * per_x, per_x)

    core_msg.wait_recv()
    x_msgs = []
    for d in (1, 2, 3):
        r = x_rows(d)
        xs[d - 1] = (gt[pl.ds(mine + r, per_x), :] + core_in[pl.ds(r, per_x), :]).astype(BF16)
        msg = message(xs.at[d - 1], xr.at[d - 1], x_away[d])
        start(msg)
        x_msgs.append(msg)
    r = x_rows(0)
    acc[...] = gt[pl.ds(mine + r, per_x), :] + core_in[pl.ds(r, per_x), :]

    pass_on(1, 2, True)
    pass_on(1, 2, False)

    def z_total(q):
        if q == 2:
            y_message(7).wait_recv()
        part = own(7, q)
        a, b = q * TILE, (q + 1) * TILE
        z_up[1, q].wait_recv()
        part = part + zru[0, a:b].astype(F32)
        z_down[1, q].wait_recv()
        return part + zrd[0, a:b].astype(F32)

    def out_rows(k, q):
        return pl.multiple_of(rows_of(k) + q_off[q], TILE)

    def finished(q, total):
        r = out_rows(0, q)
        sensors = sn[pl.ds(r, TILE), :].astype(F32)
        out[pl.ds(r, TILE), :] = (0.9 * sensors + (step_sens / math.sqrt(RANK)) * total).astype(BF16)

    g_up, g_down, g_pair = {}, {}, {}

    def hand_on(s, q):
        for upward in (True, False):
            k = (8 - (s - 1)) % 8 if upward else s - 1
            r = out_rows(k, q)
            table, who = (g_up, up) if upward else (g_down, down)
            size = TILE
            if s == 4:
                if q == 0 and not upward or q == 1 and upward:
                    continue
                if q == 2:
                    size = HALF
                    r = r if upward else r + HALF
            if s > 1:
                table[s - 1, q].wait_recv()
            rows = out.at[pl.ds(r, size)]
            table[s, q] = message(rows, rows, who)
            start(table[s, q])
            if q == 2 and (s == 1 and upward or s > 1):
                across(k, (8 - k) % 8 if k else 0)

    def across(k, label):
        r = out_rows(k, 2)
        rows = out.at[pl.ds(r, TILE)]
        g_pair[k] = message(rows, rows, pair)
        start(g_pair[k])

    pxs[...] = z_total(1).astype(BF16)
    px_msg = message(pxs, pxr, pair)
    start(px_msg)
    g[7, q_rows(0), :] = z_total(0)
    finished(2, z_total(2))
    hand_on(1, 2)

    for msg in x_msgs:
        msg.wait_recv()
    acc[...] += (xr[0].astype(F32) + xr[1].astype(F32)) + xr[2].astype(F32)
    ys[...] = acc[pl.ds(pl.multiple_of((1 - ylo) * per_y, per_y), per_y), :].astype(BF16)
    y_msg = message(ys, yr, y_next)
    start(y_msg)

    px_msg.wait_recv()
    finished(0, g[7, q_rows(0), :] + pxr[...].astype(F32))
    r0 = out_rows(0, 0)
    fin_msg = message(out.at[pl.ds(r0, TILE)], out.at[pl.ds(r0, TILE)], pair)
    start(fin_msg)
    hand_on(1, 0)
    hand_on(2, 2)

    arw_load.wait()
    rim_up.wait_recv()
    rim_down.wait_recv()
    y_msg.wait_recv()
    first = pl.multiple_of(mine + x_rows(0) + ylo * per_y, per_y)
    seen = per_y + 2 * LAG
    win = tpad[pl.ds(first, seen), :].astype(F32)
    step = first - LAG + lax.broadcasted_iota(jnp.int32, (seen, RANK), 0)
    winf[...] = jnp.where((step >= 0) | (tm > 0), win, 0.0)
    errs = per_y + LAG
    err = winf[LAG : LAG + errs, :]
    lags = (1, 12, LAG)
    for i in range(3):
        err = err - arw[i : i + 1, :] * winf[LAG - lags[i] : LAG - lags[i] + errs, :]
    step = first + lax.broadcasted_iota(jnp.int32, (errs, RANK), 0)
    errf[...] = jnp.where((step < t_rows) | (tm < 15), err, 0.0)
    adj = errf[0:per_y, :]
    for i in range(3):
        adj = adj - arw[i : i + 1, :] * errf[lags[i] : lags[i] + per_y, :]
    total = acc[pl.ds(pl.multiple_of(ylo * per_y, per_y), per_y), :] + yr[...].astype(F32)
    new = winf[LAG : LAG + per_y, :] + (step_time / math.sqrt(RANK)) * total - 0.5 * adj
    tout[pl.ds(first, per_y), :] = new.astype(BF16)
    ty_rows = tout.at[pl.ds(first, per_y)]
    ty_msg = message(ty_rows, ty_rows, y_next)
    start(ty_msg)

    fin_msg.wait_recv()
    hand_on(1, 1)
    hand_on(2, 0)
    hand_on(3, 2)
    ty_msg.wait_recv()
    tx_rows = tout.at[pl.ds(pl.multiple_of(mine + x_rows(0), per_x), per_x)]
    tx_msgs = []
    for d in (1, 2, 3):
        msg = message(tx_rows, tx_rows, x_away[d])
        start(msg)
        tx_msgs.append(msg)
    hand_on(2, 1)
    hand_on(3, 0)
    hand_on(4, 2)
    hand_on(3, 1)
    hand_on(4, 0)
    hand_on(4, 1)
    for msg in tx_msgs:
        msg.wait_recv()
    tc_rows = tout.at[pl.ds(mine, half_t)]
    tc_msg = message(tc_rows, tc_rows, other_core)
    start(tc_msg)

    g_up[4, 2].wait_recv()
    g_down[4, 2].wait_recv()
    across(4, 4)
    tc_msg.wait_recv()
    g_up[4, 0].wait_recv()
    g_down[4, 1].wait_recv()
    g_down[3, 0].wait_recv()
    g_up[3, 1].wait_recv()
    for k in (0, 7, 1, 6, 2, 5, 3, 4):
        g_pair[k].wait_recv()
    for p in range(8):
        y_message(p).wait_send()
    for msg in sent:
        msg.wait_send()


def on_device(readings, tile_mask, sensor_f, time_f, ar_weight):
    sens_here, time_here = readings.shape
    time_total = time_here * lax.axis_size("tm")
    sens_total = sens_here * lax.axis_size("blk")
    rank = sensor_f.shape[1]
    step_sens = 2.0 * math.sqrt(rank / time_total)
    step_time = 2.0 * math.sqrt(rank / sens_total)
    half_t = time_here // 2
    per_x = half_t // 4
    per_y = per_x // 2
    in_vmem = pl.BlockSpec(memory_space=pltpu.VMEM)
    messages = 100
    flops = 6 * sens_here * time_here * rank
    return pl.pallas_call(
        functools.partial(kernel, step_sens, step_time),
        out_shape=(
            pltpu.VMEM(sensor_f.shape, BF16),
            pltpu.VMEM(time_f.shape, BF16),
        ),
        in_specs=[pl.BlockSpec(memory_space=pltpu.HBM)] * 5,
        out_specs=(in_vmem, in_vmem),
        scratch_shapes=[
            pltpu.SMEM((time_here // TILE, sens_here // TILE), jnp.int32),
            pltpu.VMEM((3, rank), F32),
            pltpu.VMEM((sens_here, time_here), BF16),
            pltpu.VMEM((sens_here, rank), BF16),
            pltpu.VMEM((time_here + 2 * LAG, rank), BF16),
            pltpu.VMEM((rank, time_here), BF16),
            pltpu.VMEM((8, GROUP, rank), F32),
            pltpu.VMEM((rank, time_here), F32),
            pltpu.VMEM((rank, GROUP), BF16),
            pltpu.VMEM((GROUP, time_here), BF16),
            pltpu.VMEM((8, TILE, rank), BF16),
            pltpu.VMEM((8, TILE, rank), BF16),
            pltpu.VMEM((8, 3 * TILE, rank), BF16),
            pltpu.VMEM((4, 3 * TILE, rank), BF16),
            pltpu.VMEM((4, 3 * TILE, rank), BF16),
            pltpu.VMEM((TILE, rank), BF16),
            pltpu.VMEM((TILE, rank), BF16),
            pltpu.VMEM((time_here, rank), F32),
            pltpu.VMEM((half_t, rank), F32),
            pltpu.VMEM((3, per_x, rank), BF16),
            pltpu.VMEM((3, per_x, rank), BF16),
            pltpu.VMEM((per_x, rank), F32),
            pltpu.VMEM((per_y, rank), BF16),
            pltpu.VMEM((per_y, rank), BF16),
            pltpu.VMEM((per_y + 2 * LAG, rank), F32),
            pltpu.VMEM((per_y + LAG, rank), F32),
            pltpu.SemaphoreType.DMA((19,)),
            pltpu.SemaphoreType.DMA((messages,)),
            pltpu.SemaphoreType.DMA((messages,)),
        ],
        compiler_params=pltpu.CompilerParams(
            collective_id=0, has_side_effects=True, vmem_limit_bytes=48 * 1024 * 1024
        ),
        cost_estimate=pl.CostEstimate(
            flops=flops, bytes_accessed=2 * sens_here * time_here, transcendentals=0
        ),
        name="sweep",
    )(*[pltpu.with_memory_space_constraint(v, pltpu.HBM) for v in (readings, tile_mask.T, sensor_f, time_f, ar_weight)])


def solution(mesh):
    return jax.shard_map(
        on_device,
        mesh=mesh,
        in_specs=(P("blk", "tm"), P("blk", "tm"), P("blk", None), P("tm", None), P()),
        out_specs=(P("blk", None), P("tm", None)),
        check_vma=False,
    )
```

```python
import functools
import math

import jax
import jax.numpy as jnp
from jax import lax
from jax.experimental import pallas as pl
from jax.experimental.pallas import tpu as pltpu
from jax.sharding import PartitionSpec as P

TILE = 128
LAG = 96
RANK = 256
GROUP = 4 * TILE
HALF = 2 * TILE
PIECE = TILE // 2
COLS = 256
MESSAGES = 105
MESH = pl.DeviceIdType.MESH
F32 = jnp.float32
BF16 = jnp.bfloat16

PLACE = {4: 0, 3: 1, 5: 2, 2: 3, 6: 4, 1: 5, 7: 6, 0: 7}

ORDER = (
    "a0", "r41d0", "b0", "y01", "r40u1", "a1", "r41d1", "y00", "r40u0", "b1", "a2", "r30d0", "r31u0", "y11",
    "r31u1", "b2", "r30d1", "y21", "y20", "a3", "r31d0", "r30u1", "b3", "r42d1", "r30u0", "r31d1", "y10",
    "r42u0", "a4", "y31", "r21u0", "b4", "r32u1", "r20d0", "y41", "a5", "r21u1", "y30", "r21d0", "b5",
    "r32d1", "r20u1", "a6", "r21d1", "r32d0", "y40", "r32u0", "b6", "r20d1", "y61", "r20u0", "y51", "r11u0",
    "a7", "y50", "y60", "r11d0", "r22u1", "b7", "r22d1", "r11u1", "r11d1", "g0", "r22u0", "r22d0", "r10d0",
    "y71", "r10u0", "s10", "y70", "r12u1", "r12d1", "r10u1", "r10d1", "g1", "s11", "r12u0", "r12d0", "s00",
    "f0", "s21", "h12d1", "h12u1", "x0u1", "h10u0", "h10d0", "s01", "s20", "h12d0", "h12u0", "f1", "h10d1",
    "x0u0", "h10u1", "x1d1", "h22u1", "h22d1", "g2", "h11u0", "h11d0", "h22u0", "h22d0", "x1d0", "x1u1",
    "h20u1", "h11d1", "h20d1", "h11u1", "h32d1", "h32u1", "x2d1", "g3", "x2u1", "h21d0", "h32u0", "h20u0",
    "h21d1", "h30u1", "h32d0", "h20d0", "x2d0", "x1u0", "h21u1", "h42d1", "x3d1", "h21u0", "g4", "x2u0",
    "h42u0", "h31d0", "x3u0", "h30u0", "h31d1", "h30d1", "x3d0", "h31u1", "h30d0", "x3u1", "h31u0", "x4d1",
    "h40u1", "h41d0", "x4u0", "h40u0", "h41d1", "g5",
)


def kernel(
    step_sens, step_time,
    rd_hbm, mask_hbm, sn_hbm, t_hbm, arw_hbm,
    out, tout,
    mask, arw, rd, sn, tpad, g, gtt, resid, ysend, yrecv, zsend, zru, zrd, pxs, pxr,
    gt, core_in, xs, xr, acc, ys, yr, winf, errf,
    load_sem, send_sem, recv_sem,
):
    blk = lax.axis_index("blk")
    tm = lax.axis_index("tm")
    x, ylo, c = blk // 4, (blk // 2) % 2, blk % 2
    h, z = tm // 8, tm % 8

    def at_blk(x_, ylo_, c_):
        return ((x_ * 2 + ylo_) * 2 + c_, tm)

    up = (blk, h * 8 + (z + 1) % 8)
    down = (blk, h * 8 + (z + 7) % 8)
    pair = (blk, (1 - h) * 8 + z)
    after = (blk, (tm + 1) % 16)
    before = (blk, (tm + 15) % 16)
    other_core = at_blk(x, ylo, 1 - c)
    x_away = [None] + [at_blk((x + d) % 4, ylo, c) for d in (1, 2, 3)]
    y_next = at_blk(x, 1 - ylo, c)
    way = {"u": up, "d": down}

    barrier = pltpu.get_barrier_semaphore()
    partners = [up, down, pair, after, before, other_core, y_next] + x_away[1:]

    t_rows = t_hbm.shape[0]
    t_load = pltpu.make_async_copy(t_hbm, tpad.at[pl.ds(LAG, t_rows)], load_sem.at[16])
    mask_load = pltpu.make_async_copy(mask_hbm, mask, load_sem.at[17])
    arw_load = pltpu.make_async_copy(arw_hbm, arw, load_sem.at[18])

    def owner_of(p):
        d = (p + 1) // 2
        return (z + 8 + 4 + d * (1 - 2 * (p % 2))) % 8

    def half_rows(p, half):
        return pl.multiple_of(owner_of(p) * GROUP + half * HALF, HALF)

    def start_loads(p, half):
        r = half_rows(p, half)
        sem = load_sem.at[2 * p + half]
        pltpu.make_async_copy(sn_hbm.at[pl.ds(r, HALF)], sn.at[pl.ds(r, HALF)], sem).start()
        pltpu.make_async_copy(rd_hbm.at[pl.ds(r, HALF)], rd.at[pl.ds(r, HALF)], sem).start()

    def loaded(p, half):
        both = rd.at[pl.ds(0, HALF + HALF * RANK // t_rows)]
        pltpu.make_async_copy(both, both, load_sem.at[2 * p + half]).wait()

    t_load.start()
    start_loads(0, 0)
    mask_load.start()
    start_loads(0, 1)
    for who in partners:
        pl.semaphore_signal(barrier, inc=1, device_id=who, device_id_type=MESH)

    q_off = [h * TILE, (1 - h) * TILE, (2 + h) * TILE, (3 - h) * TILE]
    q_off = [pl.multiple_of(v, TILE) for v in q_off]

    messages, slots, landed, sent_rows = {}, {}, set(), []

    def define(name, src, dst, who, together=None):
        slot = slots.setdefault(name if together is None else together, len(slots))
        messages[name] = pltpu.make_async_remote_copy(
            src_ref=src, dst_ref=dst, send_sem=send_sem, recv_sem=recv_sem.at[slot],
            device_id=who, device_id_type=MESH,
        )

    def send(name, rows):
        messages[name].start()
        sent_rows.append(rows)

    def need(name):
        if name not in landed:
            landed.add(name)
            messages[name].wait_recv()

    def bytes_of(rows, sem):
        some = rd.at[pl.ds(0, rows * RANK // t_rows)]
        return pltpu.make_async_remote_copy(
            src_ref=some, dst_ref=some, send_sem=send_sem, recv_sem=sem, device_id=pair, device_id_type=MESH
        )

    def need_together(name, rows):
        if name not in landed:
            landed.add(name)
            bytes_of(rows, recv_sem.at[slots[name]]).wait_recv()

    def piece(q, u):
        return pl.ds(pl.multiple_of(q_off[q] + u * PIECE, PIECE), PIECE)

    def out_rows(k, q, u):
        return pl.multiple_of(((z + k) % 8) * GROUP + q_off[q] + u * PIECE, PIECE)

    def compute(p, half):
        loaded(p, half)
        r = half_rows(p, half)
        for j in range(t_rows // COLS):
            cols = slice(j * COLS, (j + 1) * COLS)
            tj = tpad[LAG + j * COLS : LAG + (j + 1) * COLS, :]
            pred = lax.dot_general(
                sn[pl.ds(r, HALF), :], tj, (((1,), (1,)), ((), ())), preferred_element_type=F32
            )
            diff = rd[pl.ds(r, HALF), cols].astype(F32) - pred * (1.0 / math.sqrt(RANK))
            for i in range(HALF // TILE):
                for jj in range(COLS // TILE):
                    tile_row = owner_of(p) * (GROUP // TILE) + half * 2 + i
                    keep = mask[j * (COLS // TILE) + jj, tile_row].astype(F32)
                    block = diff[i * TILE : (i + 1) * TILE, jj * TILE : (jj + 1) * TILE]
                    a, b = half * HALF + i * TILE, j * COLS + jj * TILE
                    resid[a : a + TILE, b : b + TILE] = (block * keep).astype(BF16)
        rows = slice(half * HALF, (half + 1) * HALF)
        g[p, rows, :] = jnp.dot(resid[rows, :], tpad[LAG : LAG + t_rows, :], preferred_element_type=F32)
        if half == 1:
            sensors = sn[pl.ds(half_rows(p, 0), GROUP), :]
            part = lax.dot_general(
                sensors, resid[...], (((0,), (0,)), ((), ())), preferred_element_type=F32
            )
            gtt[...] = part if p == 0 else gtt[...] + part

    def do_a(p):
        compute(p, 0)
        if p == 0:
            for later in range(1, 8):
                start_loads(later, 0)
                start_loads(later, 1)
            arw_load.start()
            pl.semaphore_wait(barrier, len(partners))
            define("rim_up", tpad.at[pl.ds(t_rows, LAG)], tpad.at[pl.ds(0, LAG)], after, "rims")
            define("rim_down", tpad.at[pl.ds(LAG, LAG)], tpad.at[pl.ds(LAG + t_rows, LAG)], before, "rims")

    def do_b(p):
        compute(p, 1)

    def do_y(p, u):
        rows = pl.ds(u * PIECE, PIECE)
        ysend[p, rows, :] = g[p, piece(3, u), :].astype(BF16)
        define(("y", p, u), ysend.at[p, rows], yrecv.at[p, rows], pair)
        send(("y", p, u), PIECE)

    def own(p, q, u):
        part = g[p, piece(q, u), :]
        if q == 2:
            need(("y", p, u))
            part = part + yrecv[p, pl.ds(u * PIECE, PIECE), :].astype(F32)
        return part

    def starts(k, q, d, u):
        longer = {0: "u", 1: "d", 2: "ud"[u * PIECE * 2 // TILE]}[q]
        return k == (4 if d == longer else 3)

    def do_r(k, q, d, u):
        p = PLACE[k] if d == "u" else PLACE[8 - k]
        land = zru if d == "u" else zrd
        rows = pl.ds(q * TILE + u * PIECE, PIECE)
        part = own(p, q, u)
        if not starts(k, q, d, u):
            need(("r", k + 1, q, d, u))
            part = part + land[k, rows, :].astype(F32)
        zsend[p, rows, :] = part.astype(BF16)
        define(("r", k, q, d, u), zsend.at[p, rows], land.at[k - 1, rows], way[d])
        send(("r", k, q, d, u), PIECE)

    def finished(q, u, total):
        r = out_rows(0, q, u)
        sensors = sn[pl.ds(r, PIECE), :].astype(F32)
        out[pl.ds(r, PIECE), :] = (0.9 * sensors + (step_sens / math.sqrt(RANK)) * total).astype(BF16)

    def do_s(q, u):
        rows = pl.ds(q * TILE + u * PIECE, PIECE)
        part = own(7, q, u)
        for d, land in (("u", zru), ("d", zrd)):
            need(("r", 1, q, d, u))
            part = part + land[0, rows, :].astype(F32)
        if q == 0:
            g[7, piece(0, u), :] = part
        elif q == 1:
            here = pl.ds(u * PIECE, PIECE)
            pxs[here, :] = part.astype(BF16)
            define(("s", u), pxs.at[here], pxr.at[here], pair)
            send(("s", u), PIECE)
        else:
            finished(2, u, part)

    def do_f(u):
        need(("s", u))
        finished(0, u, g[7, piece(0, u), :] + pxr[pl.ds(u * PIECE, PIECE), :].astype(F32))
        rows = out.at[pl.ds(out_rows(0, 0, u), PIECE)]
        define(("f", u), rows, rows, pair)
        send(("f", u), PIECE)

    def do_h(s, q, d, u):
        if s > 1:
            need(("h", s - 1, q, d, u))
        elif q == 1:
            need(("f", u))
        k = (9 - s) % 8 if d == "u" else s - 1
        rows = out.at[pl.ds(out_rows(k, q, u), PIECE)]
        last = s == 4 and q < 2 or s == 3 and (q == 0 and d == "d" or q == 1 and d == "u")
        define(("h", s, q, d, u), rows, rows, way[d], "last" if last else None)
        send(("h", s, q, d, u), PIECE)

    def do_x(s, d, u):
        if s > 0:
            need(("h", s, 2, d, u))
        k = (8 - s) % 8 if d == "u" else s
        rows = out.at[pl.ds(out_rows(k, 2, u), PIECE)]
        define(("x", s, d, u), rows, rows, pair, "x")
        send(("x", s, d, u), PIECE)

    half_t = t_rows // 2
    per_x = half_t // 4
    per_y = per_x // 2
    mine = pl.multiple_of(c * half_t, half_t)
    theirs = pl.multiple_of((1 - c) * half_t, half_t)
    x_rows = [pl.multiple_of(((x + d) % 4) * per_x, per_x) for d in range(4)]
    first = pl.multiple_of(mine + x_rows[0] + ylo * per_y, per_y)

    def new_time():
        arw_load.wait()
        need_together("rims", 2 * LAG)
        seen = per_y + 2 * LAG
        win = tpad[pl.ds(first, seen), :].astype(F32)
        step = first - LAG + lax.broadcasted_iota(jnp.int32, (seen, RANK), 0)
        winf[...] = jnp.where((step >= 0) | (tm > 0), win, 0.0)
        errs = per_y + LAG
        err = winf[LAG : LAG + errs, :]
        lags = (1, 12, LAG)
        for i in range(3):
            err = err - arw[i : i + 1, :] * winf[LAG - lags[i] : LAG - lags[i] + errs, :]
        step = first + lax.broadcasted_iota(jnp.int32, (errs, RANK), 0)
        errf[...] = jnp.where((step < t_rows) | (tm < 15), err, 0.0)
        adj = errf[0:per_y, :]
        for i in range(3):
            adj = adj - arw[i : i + 1, :] * errf[lags[i] : lags[i] + per_y, :]
        total = acc[pl.ds(pl.multiple_of(ylo * per_y, per_y), per_y), :] + yr[...].astype(F32)
        new = winf[LAG : LAG + per_y, :] + (step_time / math.sqrt(RANK)) * total - 0.5 * adj
        tout[pl.ds(first, per_y), :] = new.astype(BF16)

    def do_g(n):
        if n == 0:
            send("rim_up", LAG)
            send("rim_down", LAG)
            for j in range(t_rows // COLS):
                gt[j * COLS : (j + 1) * COLS, :] = gtt[:, j * COLS : (j + 1) * COLS].T
            define("core", gt.at[pl.ds(theirs, half_t)], core_in, other_core)
            send("core", 2 * half_t)
        elif n == 1:
            need("core")
            for d in (1, 2, 3):
                rows = x_rows[d]
                total = gt[pl.ds(mine + rows, per_x), :] + core_in[pl.ds(rows, per_x), :]
                xs[d - 1] = total.astype(BF16)
                define(("gx", d), xs.at[d - 1], xr.at[d - 1], x_away[d], "gx")
                send(("gx", d), per_x)
            rows = x_rows[0]
            acc[...] = gt[pl.ds(mine + rows, per_x), :] + core_in[pl.ds(rows, per_x), :]
        elif n == 2:
            need_together("gx", 3 * per_x)
            acc[...] += (xr[0].astype(F32) + xr[1].astype(F32)) + xr[2].astype(F32)
            ys[...] = acc[pl.ds(pl.multiple_of((1 - ylo) * per_y, per_y), per_y), :].astype(BF16)
            define("gy", ys, yr, y_next)
            send("gy", per_y)
        elif n == 3:
            need("gy")
            new_time()
            rows = tout.at[pl.ds(first, per_y)]
            define("ty", rows, rows, y_next)
            send("ty", per_y)
        elif n == 4:
            need("ty")
            rows = tout.at[pl.ds(pl.multiple_of(mine + x_rows[0], per_x), per_x)]
            for d in (1, 2, 3):
                define(("tx", d), rows, rows, x_away[d], "tx")
                send(("tx", d), per_x)
        else:
            need_together("tx", 3 * per_x)
            rows = tout.at[pl.ds(mine, half_t)]
            define("tc", rows, rows, other_core)
            send("tc", half_t)

    t_load.wait()
    mask_load.wait()
    todo = {
        "a": do_a, "b": do_b, "y": do_y, "r": do_r, "s": do_s, "f": do_f, "h": do_h, "x": do_x, "g": do_g
    }
    for step in ORDER:
        todo[step[0]](*(v if v in "ud" else int(v) for v in step[1:]))
    need("tc")
    need_together("x", 8 * TILE)
    need_together("last", 4 * TILE)
    assert all(name in landed for name in slots)
    bytes_of(sum(sent_rows), recv_sem.at[0]).wait_send()


def write_out(new_sensor, new_time, sensor_hbm, time_hbm, sem):
    a = pltpu.make_async_copy(new_sensor, sensor_hbm, sem.at[0])
    b = pltpu.make_async_copy(new_time, time_hbm, sem.at[1])
    a.start()
    b.start()
    a.wait()
    b.wait()


def on_device(readings, tile_mask, sensor_f, time_f, ar_weight):
    sens_here, time_here = readings.shape
    time_total = time_here * lax.axis_size("tm")
    sens_total = sens_here * lax.axis_size("blk")
    rank = sensor_f.shape[1]
    step_sens = 2.0 * math.sqrt(rank / time_total)
    step_time = 2.0 * math.sqrt(rank / sens_total)
    half_t = time_here // 2
    per_x = half_t // 4
    per_y = per_x // 2
    in_vmem = pl.BlockSpec(memory_space=pltpu.VMEM)
    flops = 6 * sens_here * time_here * rank
    operands = (readings, tile_mask.T, sensor_f, time_f, ar_weight)
    new_sensor, new_time = pl.pallas_call(
        functools.partial(kernel, step_sens, step_time),
        out_shape=(
            pltpu.VMEM(sensor_f.shape, BF16),
            pltpu.VMEM(time_f.shape, BF16),
        ),
        in_specs=[pl.BlockSpec(memory_space=pltpu.HBM)] * 5,
        out_specs=(in_vmem, in_vmem),
        scratch_shapes=[
            pltpu.SMEM((time_here // TILE, sens_here // TILE), jnp.int32),
            pltpu.VMEM((3, rank), F32),
            pltpu.VMEM((sens_here, time_here), BF16),
            pltpu.VMEM((sens_here, rank), BF16),
            pltpu.VMEM((time_here + 2 * LAG, rank), BF16),
            pltpu.VMEM((8, GROUP, rank), F32),
            pltpu.VMEM((rank, time_here), F32),
            pltpu.VMEM((GROUP, time_here), BF16),
            pltpu.VMEM((8, TILE, rank), BF16),
            pltpu.VMEM((8, TILE, rank), BF16),
            pltpu.VMEM((8, 3 * TILE, rank), BF16),
            pltpu.VMEM((4, 3 * TILE, rank), BF16),
            pltpu.VMEM((4, 3 * TILE, rank), BF16),
            pltpu.VMEM((TILE, rank), BF16),
            pltpu.VMEM((TILE, rank), BF16),
            pltpu.VMEM((time_here, rank), F32),
            pltpu.VMEM((half_t, rank), F32),
            pltpu.VMEM((3, per_x, rank), BF16),
            pltpu.VMEM((3, per_x, rank), BF16),
            pltpu.VMEM((per_x, rank), F32),
            pltpu.VMEM((per_y, rank), BF16),
            pltpu.VMEM((per_y, rank), BF16),
            pltpu.VMEM((per_y + 2 * LAG, rank), F32),
            pltpu.VMEM((per_y + LAG, rank), F32),
            pltpu.SemaphoreType.DMA((19,)),
            pltpu.SemaphoreType.DMA,
            pltpu.SemaphoreType.DMA((MESSAGES,)),
        ],
        compiler_params=pltpu.CompilerParams(
            collective_id=0, has_side_effects=True, vmem_limit_bytes=48 * 1024 * 1024
        ),
        cost_estimate=pl.CostEstimate(
            flops=flops, bytes_accessed=2 * sens_here * time_here, transcendentals=0
        ),
        name="sweep",
    )(*[pltpu.with_memory_space_constraint(v, pltpu.HBM) for v in operands])
    in_hbm = pl.BlockSpec(memory_space=pltpu.HBM)
    return pl.pallas_call(
        write_out,
        out_shape=(pltpu.HBM(sensor_f.shape, BF16), pltpu.HBM(time_f.shape, BF16)),
        in_specs=[in_vmem, in_vmem],
        out_specs=(in_hbm, in_hbm),
        scratch_shapes=[pltpu.SemaphoreType.DMA((2,))],
        name="write_out",
    )(*[pltpu.with_memory_space_constraint(v, pltpu.VMEM) for v in (new_sensor, new_time)])


def solution(mesh):
    return jax.shard_map(
        on_device,
        mesh=mesh,
        in_specs=(P("blk", "tm"), P("blk", "tm"), P("blk", None), P("tm", None), P()),
        out_specs=(P("blk", None), P("tm", None)),
        check_vma=False,
    )
```

```python
import functools
import math

import jax
import jax.numpy as jnp
from jax import lax
from jax.experimental import pallas as pl
from jax.experimental.pallas import tpu as pltpu
from jax.sharding import PartitionSpec as P

TILE = 128
LAG = 96
RANK = 256
GROUP = 4 * TILE
HALF = 2 * TILE
PIECE = TILE // 2
COLS = 256
Y_PIECES = 2
MESSAGES = 98
MESH = pl.DeviceIdType.MESH
F32 = jnp.float32
BF16 = jnp.bfloat16

PLACE = {4: 0, 3: 1, 5: 2, 2: 3, 6: 4, 1: 5, 7: 6, 0: 7}

ORDER = (
    "a0", "r41d0", "b0", "y01", "r40u1", "a1", "r41d1", "y00", "r40u0", "b1", "a2", "r30d0", "r31u0", "y11",
    "r31u1", "b2", "r30d1", "y21", "a3", "r31d0", "r30u1", "b3", "r42d1", "r30u0", "r31d1",
    "r42u0", "a4", "y31", "r21u0", "b4", "r32u1", "r20d0", "y41", "a5", "r21u1", "r21d0", "b5",
    "r32d1", "r20u1", "a6", "r21d1", "r32d0", "r32u0", "b6", "r20d1", "y61", "r20u0", "y51", "r11u0",
    "a7", "r11d0", "r22u1", "b7", "r22d1", "r11u1", "r11d1", "g0", "r22u0", "r22d0", "r10d0",
    "y71", "r10u0", "s10", "r12u1", "r12d1", "r10u1", "r10d1", "g1", "s11", "r12u0", "r12d0", "s00",
    "f0", "s21", "h12d1", "h12u1", "x0u1", "h10u0", "h10d0", "s01", "s20", "h12d0", "h12u0", "f1", "h10d1",
    "x0u0", "h10u1", "x1d1", "h22u1", "h22d1", "g2", "h11u0", "h11d0", "h22u0", "h22d0", "x1d0", "x1u1",
    "h20u1", "h11d1", "h20d1", "h11u1", "h32d1", "h32u1", "x2d1", "g3", "x2u1", "h21d0", "h32u0", "h20u0",
    "h21d1", "h30u1", "h32d0", "h20d0", "x2d0", "x1u0", "h21u1", "h42d1", "x3d1", "h21u0", "g4", "x2u0",
    "h42u0", "h31d0", "x3u0", "h30u0", "h31d1", "h30d1", "x3d0", "h31u1", "h30d0", "x3u1", "h31u0", "x4d1",
    "h40u1", "h41d0", "x4u0", "h40u0", "h41d1", "g5",
)


def kernel(
    step_sens, step_time,
    rd_hbm, mask_hbm, sn_hbm, t_hbm, arw_hbm,
    out, tout,
    mask, arw, rd, sn, tpad, g, gtt, resid, ysend, yrecv, zsend, zru, zrd, pxs, pxr,
    gt, core_in, xs, xr, acc, ys, yr, winf, errf,
    load_sem, send_sem, recv_sem,
):
    blk = lax.axis_index("blk")
    tm = lax.axis_index("tm")
    x, ylo, c = blk // 4, (blk // 2) % 2, blk % 2
    h, z = tm // 8, tm % 8

    def at_blk(x_, ylo_, c_):
        return ((x_ * 2 + ylo_) * 2 + c_, tm)

    up = (blk, h * 8 + (z + 1) % 8)
    down = (blk, h * 8 + (z + 7) % 8)
    pair = (blk, (1 - h) * 8 + z)
    after = (blk, (tm + 1) % 16)
    before = (blk, (tm + 15) % 16)
    other_core = at_blk(x, ylo, 1 - c)
    x_away = [None] + [at_blk((x + d) % 4, ylo, c) for d in (1, 2, 3)]
    y_next = at_blk(x, 1 - ylo, c)
    way = {"u": up, "d": down}

    barrier = pltpu.get_barrier_semaphore()
    partners = [up, down, pair, after, before, other_core, y_next] + x_away[1:]

    t_rows = t_hbm.shape[0]
    t_load = pltpu.make_async_copy(t_hbm, tpad.at[pl.ds(LAG, t_rows)], load_sem.at[16])
    mask_load = pltpu.make_async_copy(mask_hbm, mask, load_sem.at[17])
    arw_load = pltpu.make_async_copy(arw_hbm, arw, load_sem.at[18])

    def owner_of(p):
        d = (p + 1) // 2
        return (z + 8 + 4 + d * (1 - 2 * (p % 2))) % 8

    def half_rows(p, half):
        return pl.multiple_of(owner_of(p) * GROUP + half * HALF, HALF)

    def start_loads(p, half):
        r = half_rows(p, half)
        sem = load_sem.at[2 * p + half]
        pltpu.make_async_copy(sn_hbm.at[pl.ds(r, HALF)], sn.at[pl.ds(r, HALF)], sem).start()
        pltpu.make_async_copy(rd_hbm.at[pl.ds(r, HALF)], rd.at[pl.ds(r, HALF)], sem).start()

    def loaded(p, half):
        both = rd.at[pl.ds(0, HALF + HALF * RANK // t_rows)]
        pltpu.make_async_copy(both, both, load_sem.at[2 * p + half]).wait()

    t_load.start()
    start_loads(0, 0)
    mask_load.start()
    start_loads(0, 1)
    for who in partners:
        pl.semaphore_signal(barrier, inc=1, device_id=who, device_id_type=MESH)

    q_off = [h * TILE, (1 - h) * TILE, (2 + h) * TILE, (3 - h) * TILE]
    q_off = [pl.multiple_of(v, TILE) for v in q_off]

    messages, slots, landed, sent_rows = {}, {}, set(), []

    def arrival(name):
        return recv_sem.at[slots.setdefault(name, len(slots))]

    def define(name, src, dst, who, together=None):
        messages[name] = pltpu.make_async_remote_copy(
            src_ref=src, dst_ref=dst, send_sem=send_sem, recv_sem=arrival(name if together is None else together),
            device_id=who, device_id_type=MESH,
        )

    def send(name, rows):
        messages[name].start()
        sent_rows.append(rows)

    def bytes_of(rows, sem):
        some = rd.at[pl.ds(0, rows * RANK // t_rows)]
        return pltpu.make_async_remote_copy(
            src_ref=some, dst_ref=some, send_sem=send_sem, recv_sem=sem, device_id=pair, device_id_type=MESH
        )

    def need(name, rows=PIECE):
        if name not in landed:
            landed.add(name)
            bytes_of(rows, arrival(name)).wait_recv()

    def piece(q, u):
        return pl.ds(pl.multiple_of(q_off[q] + u * PIECE, PIECE), PIECE)

    def out_rows(k, q, u):
        return pl.multiple_of(((z + k) % 8) * GROUP + q_off[q] + u * PIECE, PIECE)

    def compute(p, half):
        loaded(p, half)
        r = half_rows(p, half)
        for j in range(t_rows // COLS):
            cols = slice(j * COLS, (j + 1) * COLS)
            tj = tpad[LAG + j * COLS : LAG + (j + 1) * COLS, :]
            pred = lax.dot_general(
                sn[pl.ds(r, HALF), :], tj, (((1,), (1,)), ((), ())), preferred_element_type=F32
            )
            diff = rd[pl.ds(r, HALF), cols].astype(F32) - pred * (1.0 / math.sqrt(RANK))
            for i in range(HALF // TILE):
                for jj in range(COLS // TILE):
                    tile_row = owner_of(p) * (GROUP // TILE) + half * 2 + i
                    keep = mask[j * (COLS // TILE) + jj, tile_row].astype(F32)
                    block = diff[i * TILE : (i + 1) * TILE, jj * TILE : (jj + 1) * TILE]
                    a, b = half * HALF + i * TILE, j * COLS + jj * TILE
                    resid[a : a + TILE, b : b + TILE] = (block * keep).astype(BF16)
        rows = slice(half * HALF, (half + 1) * HALF)
        g[p, rows, :] = jnp.dot(resid[rows, :], tpad[LAG : LAG + t_rows, :], preferred_element_type=F32)
        if half == 1:
            sensors = sn[pl.ds(half_rows(p, 0), GROUP), :]
            part = lax.dot_general(
                sensors, resid[...], (((0,), (0,)), ((), ())), preferred_element_type=F32
            )
            gtt[...] += part

    def begin():
        for later in range(1, 8):
            start_loads(later, 0)
            start_loads(later, 1)
        arw_load.start()
        pl.semaphore_wait(barrier, len(partners))

    def do_y(p, u):
        u = u if p == 0 else 0
        size = TILE // Y_PIECES if p == 0 else TILE
        rows = pl.ds(u * size, size)
        part = g[p, pl.ds(pl.multiple_of(q_off[3] + u * size, size), size), :]
        ysend[p, rows, :] = part.astype(BF16)
        define(("y", p, u), ysend.at[p, rows], yrecv.at[p, rows], pair)
        send(("y", p, u), size)

    def own(p, q, u):
        part = g[p, piece(q, u), :]
        if q == 2:
            if p == 0:
                need(("y", p, u * PIECE * Y_PIECES // TILE), TILE // Y_PIECES)
            elif u == 1:
                need(("y", p, 0), TILE)
            part = part + yrecv[p, pl.ds(u * PIECE, PIECE), :].astype(F32)
        return part

    def starts(k, q, d, u):
        longer = {0: "u", 1: "d", 2: "ud"[u * PIECE * 2 // TILE]}[q]
        return k == (4 if d == longer else 3)

    def do_r(k, q, d, u):
        p = PLACE[k] if d == "u" else PLACE[8 - k]
        land = zru if d == "u" else zrd
        rows = pl.ds(q * TILE + u * PIECE, PIECE)
        part = own(p, q, u)
        if not starts(k, q, d, u):
            need(("r", k + 1, q, d, u))
            part = part + land[k, rows, :].astype(F32)
        zsend[p, rows, :] = part.astype(BF16)
        define(("r", k, q, d, u), zsend.at[p, rows], land.at[k - 1, rows], way[d])
        send(("r", k, q, d, u), PIECE)

    def finished(q, u, total):
        r = out_rows(0, q, u)
        sensors = sn[pl.ds(r, PIECE), :].astype(F32)
        out[pl.ds(r, PIECE), :] = (0.9 * sensors + (step_sens / math.sqrt(RANK)) * total).astype(BF16)

    def do_s(q, u):
        rows = pl.ds(q * TILE + u * PIECE, PIECE)
        part = own(7, q, u)
        for d, land in (("u", zru), ("d", zrd)):
            need(("r", 1, q, d, u))
            part = part + land[0, rows, :].astype(F32)
        if q == 0:
            g[7, piece(0, u), :] = part
        elif q == 1:
            here = pl.ds(u * PIECE, PIECE)
            pxs[here, :] = part.astype(BF16)
            define(("s", u), pxs.at[here], pxr.at[here], pair)
            send(("s", u), PIECE)
        else:
            finished(2, u, part)

    def do_f(u):
        need(("s", u))
        finished(0, u, g[7, piece(0, u), :] + pxr[pl.ds(u * PIECE, PIECE), :].astype(F32))
        rows = out.at[pl.ds(out_rows(0, 0, u), PIECE)]
        define(("f", u), rows, rows, pair)
        send(("f", u), PIECE)

    def do_h(s, q, d, u):
        if s > 1:
            need(("h", s - 1, q, d, u))
        elif q == 1:
            need(("f", u))
        k = (9 - s) % 8 if d == "u" else s - 1
        rows = out.at[pl.ds(out_rows(k, q, u), PIECE)]
        last = s == 4 and q < 2 or s == 3 and (q == 0 and d == "d" or q == 1 and d == "u")
        define(("h", s, q, d, u), rows, rows, way[d], "last" if last else None)
        send(("h", s, q, d, u), PIECE)

    def do_x(s, d, u):
        if s > 0:
            need(("h", s, 2, d, u))
        k = (8 - s) % 8 if d == "u" else s
        rows = out.at[pl.ds(out_rows(k, 2, u), PIECE)]
        define(("x", s, d, u), rows, rows, pair, "x")
        send(("x", s, d, u), PIECE)

    half_t = t_rows // 2
    per_x = half_t // 4
    per_y = per_x // 2
    mine = pl.multiple_of(c * half_t, half_t)
    theirs = pl.multiple_of((1 - c) * half_t, half_t)
    x_rows = [pl.multiple_of(((x + d) % 4) * per_x, per_x) for d in range(4)]
    first = pl.multiple_of(mine + x_rows[0] + ylo * per_y, per_y)

    def new_time():
        arw_load.wait()
        need("rims", 2 * LAG)
        seen = per_y + 2 * LAG
        win = tpad[pl.ds(first, seen), :].astype(F32)
        step = first - LAG + lax.broadcasted_iota(jnp.int32, (seen, RANK), 0)
        winf[...] = jnp.where((step >= 0) | (tm > 0), win, 0.0)
        errs = per_y + LAG
        err = winf[LAG : LAG + errs, :]
        lags = (1, 12, LAG)
        for i in range(3):
            err = err - arw[i : i + 1, :] * winf[LAG - lags[i] : LAG - lags[i] + errs, :]
        step = first + lax.broadcasted_iota(jnp.int32, (errs, RANK), 0)
        errf[...] = jnp.where((step < t_rows) | (tm < 15), err, 0.0)
        adj = errf[0:per_y, :]
        for i in range(3):
            adj = adj - arw[i : i + 1, :] * errf[lags[i] : lags[i] + per_y, :]
        total = acc[pl.ds(pl.multiple_of(ylo * per_y, per_y), per_y), :] + yr[...].astype(F32)
        new = winf[LAG : LAG + per_y, :] + (step_time / math.sqrt(RANK)) * total - 0.5 * adj
        tout[pl.ds(first, per_y), :] = new.astype(BF16)

    def do_g(n):
        if n == 0:
            define("rim_up", tpad.at[pl.ds(t_rows, LAG)], tpad.at[pl.ds(0, LAG)], after, "rims")
            define("rim_down", tpad.at[pl.ds(LAG, LAG)], tpad.at[pl.ds(LAG + t_rows, LAG)], before, "rims")
            send("rim_up", LAG)
            send("rim_down", LAG)
            for j in range(t_rows // COLS):
                gt[j * COLS : (j + 1) * COLS, :] = gtt[:, j * COLS : (j + 1) * COLS].T
            define("core", gt.at[pl.ds(theirs, half_t)], core_in, other_core)
            send("core", 2 * half_t)
        elif n == 1:
            need("core", 2 * half_t)
            for d in (1, 2, 3):
                rows = x_rows[d]
                total = gt[pl.ds(mine + rows, per_x), :] + core_in[pl.ds(rows, per_x), :]
                xs[d - 1] = total.astype(BF16)
                define(("gx", d), xs.at[d - 1], xr.at[d - 1], x_away[d], "gx")
                send(("gx", d), per_x)
            rows = x_rows[0]
            acc[...] = gt[pl.ds(mine + rows, per_x), :] + core_in[pl.ds(rows, per_x), :]
        elif n == 2:
            need("gx", 3 * per_x)
            acc[...] += (xr[0].astype(F32) + xr[1].astype(F32)) + xr[2].astype(F32)
            ys[...] = acc[pl.ds(pl.multiple_of((1 - ylo) * per_y, per_y), per_y), :].astype(BF16)
            define("gy", ys, yr, y_next)
            send("gy", per_y)
        elif n == 3:
            need("gy", per_y)
            new_time()
            rows = tout.at[pl.ds(first, per_y)]
            define("ty", rows, rows, y_next)
            send("ty", per_y)
        elif n == 4:
            need("ty", per_y)
            rows = tout.at[pl.ds(pl.multiple_of(mine + x_rows[0], per_x), per_x)]
            for d in (1, 2, 3):
                define(("tx", d), rows, rows, x_away[d], "tx")
                send(("tx", d), per_x)
        else:
            need("tx", 3 * per_x)
            rows = tout.at[pl.ds(mine, half_t)]
            define("tc", rows, rows, other_core)
            send("tc", half_t)

    todo = {"y": do_y, "r": do_r, "s": do_s, "f": do_f, "h": do_h, "x": do_x, "g": do_g}

    def run(steps):
        for step in steps:
            if step == "a0":
                begin()
            elif step[0] not in "ab":
                todo[step[0]](*(v if v in "ud" else int(v) for v in step[1:]))

    def run_one(p, low, parts):
        if len(parts) == 1:
            run(parts[0])
        else:
            middle = len(parts) // 2

            @pl.when(p < low + middle)
            def _():
                run_one(p, low, parts[:middle])

            @pl.when(p >= low + middle)
            def _():
                run_one(p, low + middle, parts[middle:])

    starts_at = [ORDER.index(half + str(p)) for p in range(8) for half in "ab"]
    parts = [ORDER[i:j] for i, j in zip(starts_at, starts_at[1:] + [len(ORDER)])]
    parts, rest = parts[:15] + [()], parts[15]
    gtt[...] = jnp.zeros_like(gtt)
    t_load.wait()
    mask_load.wait()

    def group(p, carry):
        compute(p, 0)
        run_one(p, 0, parts[0::2])
        compute(p, 1)
        run_one(p, 0, parts[1::2])
        return carry

    lax.fori_loop(0, 8, group, 0)
    run(rest)
    need("tc", half_t)
    need("x", 8 * TILE)
    need("last", 4 * TILE)
    assert all(name in landed for name in slots)
    bytes_of(sum(sent_rows), recv_sem.at[0]).wait_send()


def write_out(new_sensor, new_time, sensor_hbm, time_hbm, sem):
    a = pltpu.make_async_copy(new_sensor, sensor_hbm, sem.at[0])
    b = pltpu.make_async_copy(new_time, time_hbm, sem.at[1])
    a.start()
    b.start()
    a.wait()
    b.wait()


def on_device(readings, tile_mask, sensor_f, time_f, ar_weight):
    sens_here, time_here = readings.shape
    time_total = time_here * lax.axis_size("tm")
    sens_total = sens_here * lax.axis_size("blk")
    rank = sensor_f.shape[1]
    step_sens = 2.0 * math.sqrt(rank / time_total)
    step_time = 2.0 * math.sqrt(rank / sens_total)
    half_t = time_here // 2
    per_x = half_t // 4
    per_y = per_x // 2
    in_vmem = pl.BlockSpec(memory_space=pltpu.VMEM)
    flops = 6 * sens_here * time_here * rank
    operands = (readings, tile_mask.T, sensor_f, time_f, ar_weight)
    new_sensor, new_time = pl.pallas_call(
        functools.partial(kernel, step_sens, step_time),
        out_shape=(
            pltpu.VMEM(sensor_f.shape, BF16),
            pltpu.VMEM(time_f.shape, BF16),
        ),
        in_specs=[pl.BlockSpec(memory_space=pltpu.HBM)] * 5,
        out_specs=(in_vmem, in_vmem),
        scratch_shapes=[
            pltpu.SMEM((time_here // TILE, sens_here // TILE), jnp.int32),
            pltpu.VMEM((3, rank), F32),
            pltpu.VMEM((sens_here, time_here), BF16),
            pltpu.VMEM((sens_here, rank), BF16),
            pltpu.VMEM((time_here + 2 * LAG, rank), BF16),
            pltpu.VMEM((8, GROUP, rank), F32),
            pltpu.VMEM((rank, time_here), F32),
            pltpu.VMEM((GROUP, time_here), BF16),
            pltpu.VMEM((8, TILE, rank), BF16),
            pltpu.VMEM((8, TILE, rank), BF16),
            pltpu.VMEM((8, 3 * TILE, rank), BF16),
            pltpu.VMEM((4, 3 * TILE, rank), BF16),
            pltpu.VMEM((4, 3 * TILE, rank), BF16),
            pltpu.VMEM((TILE, rank), BF16),
            pltpu.VMEM((TILE, rank), BF16),
            pltpu.VMEM((time_here, rank), F32),
            pltpu.VMEM((half_t, rank), F32),
            pltpu.VMEM((3, per_x, rank), BF16),
            pltpu.VMEM((3, per_x, rank), BF16),
            pltpu.VMEM((per_x, rank), F32),
            pltpu.VMEM((per_y, rank), BF16),
            pltpu.VMEM((per_y, rank), BF16),
            pltpu.VMEM((per_y + 2 * LAG, rank), F32),
            pltpu.VMEM((per_y + LAG, rank), F32),
            pltpu.SemaphoreType.DMA((19,)),
            pltpu.SemaphoreType.DMA,
            pltpu.SemaphoreType.DMA((MESSAGES,)),
        ],
        compiler_params=pltpu.CompilerParams(
            collective_id=0, has_side_effects=True, vmem_limit_bytes=48 * 1024 * 1024
        ),
        cost_estimate=pl.CostEstimate(
            flops=flops, bytes_accessed=2 * sens_here * time_here, transcendentals=0
        ),
        name="sweep",
    )(*[pltpu.with_memory_space_constraint(v, pltpu.HBM) for v in operands])
    in_hbm = pl.BlockSpec(memory_space=pltpu.HBM)
    return pl.pallas_call(
        write_out,
        out_shape=(pltpu.HBM(sensor_f.shape, BF16), pltpu.HBM(time_f.shape, BF16)),
        in_specs=[in_vmem, in_vmem],
        out_specs=(in_hbm, in_hbm),
        scratch_shapes=[pltpu.SemaphoreType.DMA((2,))],
        name="write_out",
    )(*[pltpu.with_memory_space_constraint(v, pltpu.VMEM) for v in (new_sensor, new_time)])


def solution(mesh):
    return jax.shard_map(
        on_device,
        mesh=mesh,
        in_specs=(P("blk", "tm"), P("blk", "tm"), P("blk", None), P("tm", None), P()),
        out_specs=(P("blk", None), P("tm", None)),
        check_vma=False,
    )
```
